32 devices in a mesh: frame: 4 (over y, x), pos: 8 (over z, core).
Axes of the slice: x: 2, y: 2, z: 4, core: 2. Of those that a mesh axis runs over, the one named last changes fastest.
Arguments:
- frames_in: bfloat16 [256, 256, 512], P('frame', 'pos'), may hold values from -40 to 40
- attn_gain: float32 [512], replicated, may hold values from 0.5 to 1.5
- w_query: bfloat16 [512, 512], replicated, may hold values from -4 to 4
- w_key: bfloat16 [512, 512], replicated, may hold values from -4 to 4
- w_value: bfloat16 [512, 512], replicated, may hold values from -0.25 to 0.25
- w_output: bfloat16 [512, 512], replicated, may hold values from -0.25 to 0.25
- moe_gain: float32 [512], replicated, may hold values from 0.5 to 1.5
- dispatch_keys: bfloat16 [512, 1024], replicated, may hold values from -10 to 10
- w_in: bfloat16 [16, 512, 2048], P('pos'), may hold values from -0.25 to 0.25
- w_out: bfloat16 [16, 2048, 512], P('pos'), may hold values from -0.125 to 0.125
Outputs:
- frames_out: bfloat16 [256, 256, 512], P('frame', 'pos')
The draws below stay inside these ranges and needn't reach their ends.
All inputs are finite; a program needn't handle non-finite values.
Results may differ from the reference program's by a relative error of at most 0.0052.
Values may be sent and summed in bfloat16 or wider, within the bound.
A program may use at most 64 MiB of HBM per device.

```python
import jax
import jax.numpy as jnp
from jax import lax

FR_DEV = 64
POSITIONS = 256
D = 512
HEADS = 8
EXPERTS = 16
SLOTS = 64
EXPERT_FF = 2048
SPLITS = 1
N_FRAME = 4


def draw_frames_in(key, part):
    array_shape = (FR_DEV * N_FRAME, POSITIONS, D)
    drawn = jax.random.normal(jax.random.fold_in(key, 1), array_shape, jnp.float32)
    return jnp.clip(drawn, -40.0, 40.0).astype(jnp.bfloat16)


def projection_draw(key, salt):
    baseline = jax.random.normal(jax.random.fold_in(key, salt), (D, D), jnp.float32) / jnp.sqrt(float(D))
    return jnp.clip(baseline, -4.0, 4.0).astype(jnp.bfloat16)


def draw_w_query(key, part):
    return projection_draw(key, 11)


def draw_w_key(key, part):
    return projection_draw(key, 12)


def draw_dispatch_keys(key, part):
    columns = EXPERTS * SLOTS
    baseline = jax.random.normal(jax.random.fold_in(key, 21), (D, columns), jnp.float32) / jnp.sqrt(float(D))
    return jnp.clip(baseline, -10.0, 10.0).astype(jnp.bfloat16)


def block_scale(key, extent, split, low, high):
    factor_of = 1.0
    for position, shards_of in split:
        draws = jax.random.uniform(jax.random.fold_in(jax.random.fold_in(key, 6), position), (shards_of,), jnp.float32, low / len(split), high / len(split))
        factor_of = factor_of * jnp.repeat(jnp.exp(draws), extent[position] // shards_of).reshape((-1,) + (1,) * (len(extent) - 1 - position))
    return factor_of


def normal_values(own_key, extent, deviation, limit, split=(), kind=jnp.bfloat16):
    factor_of = block_scale(own_key, extent, split, -0.22, 0.18) if split else 1.0
    array = jax.random.normal(own_key, extent, jnp.float32) * deviation * factor_of
    return jnp.minimum(jnp.maximum(array, -limit), limit).astype(kind)


def setup_inputs(seed: int = 0) -> dict:
    key_of = jax.random.split(jax.random.key(seed), 11)
    return {
        "frames_in": draw_frames_in(jax.random.fold_in(key_of[10], 71), 0),
        "attn_gain": jnp.clip(1.0 + 0.1 * jax.random.normal(key_of[1], (D,), jnp.float32), 0.5, 1.5),
        "w_query": draw_w_query(jax.random.fold_in(key_of[10], 71), 0),
        "w_key": draw_w_key(jax.random.fold_in(key_of[10], 71), 0),
        "w_value": normal_values(key_of[4], (D, D), D ** -0.5, 0.25),
        "w_output": normal_values(key_of[5], (D, D), D ** -0.5, 0.25),
        "moe_gain": jnp.clip(1.0 + 0.1 * jax.random.normal(key_of[6], (D,), jnp.float32), 0.5, 1.5),
        "dispatch_keys": draw_dispatch_keys(jax.random.fold_in(key_of[10], 71), 0),
        "w_in": normal_values(key_of[8], (EXPERTS * SPLITS, D, EXPERT_FF // SPLITS), D ** -0.5, 0.25, ((0, 8),)),
        "w_out": normal_values(key_of[9], (EXPERTS * SPLITS, EXPERT_FF // SPLITS, D), EXPERT_FF ** -0.5, 0.125, ((0, 8),)),
    }


EPS = 1e-06
LOGIT_SCALE = 3.0
MASKED = -1e+30

def rms_scale(values_in, gain):
    values_in = values_in.astype(jnp.float32)
    mean_sq = lax.optimization_barrier(jnp.mean(values_in * values_in, axis=-1, keepdims=True))
    return values_in * lax.rsqrt(mean_sq + EPS) * gain.astype(jnp.float32)

def project(rows_in, weights):
    return jnp.dot(rows_in, weights, preferred_element_type=jnp.float32).astype(jnp.bfloat16)

def softmax_rows(scores, axis_index):
    largest = lax.optimization_barrier(jnp.max(scores, axis=axis_index, keepdims=True))
    weights = jnp.exp(scores - largest)
    return (weights / lax.optimization_barrier(jnp.sum(weights, axis=axis_index, keepdims=True))).astype(jnp.bfloat16)

def reference(frames_in, attn_gain, w_query, w_key, w_value, w_output, moe_gain, dispatch_keys, w_in, w_out):
    frame_count, pos_count, features = frames_in.shape
    head_dim = features // HEADS
    score_scale = head_dim ** (-0.5)
    normed = rms_scale(frames_in, attn_gain).astype(jnp.bfloat16).reshape(frame_count * pos_count, features)
    shaped = (frame_count, pos_count, HEADS, head_dim)
    queries = project(normed, w_query).reshape(shaped).transpose(1, 0, 2, 3)
    keys_block = project(normed, w_key).reshape(shaped).transpose(1, 0, 2, 3)
    values_block = project(normed, w_value).reshape(shaped).transpose(1, 0, 2, 3)
    causal = jnp.arange(frame_count)[:, None] >= jnp.arange(frame_count)[None, :]

    def per_position(triple):
        queries_pos, keys_pos, values_pos = triple
        scores = jnp.einsum('fhd,ghd->hfg', queries_pos.astype(jnp.float32), keys_pos.astype(jnp.float32)) * score_scale
        scores = jnp.where(causal[None], scores, MASKED)
        attention = softmax_rows(scores, 2)
        return jnp.einsum('hfg,ghd->fhd', attention.astype(jnp.float32), values_pos.astype(jnp.float32)).astype(jnp.bfloat16)
    mixed_heads = lax.map(per_position, (queries, keys_block, values_block))
    mixed_heads = mixed_heads.transpose(1, 0, 2, 3).reshape(frame_count * pos_count, features)
    residual = (frames_in.reshape(frame_count * pos_count, features).astype(jnp.float32) + jnp.dot(mixed_heads, w_output, preferred_element_type=jnp.float32)).astype(jnp.bfloat16)
    moe_input = rms_scale(residual, moe_gain).astype(jnp.bfloat16)
    blocks = moe_input.reshape(frame_count // FR_DEV, FR_DEV * pos_count, features)
    splits = w_in.shape[0] // EXPERTS

    def per_block(block_rows):
        logits = LOGIT_SCALE * jnp.dot(block_rows, dispatch_keys, preferred_element_type=jnp.float32)
        dispatch = softmax_rows(logits, 0)
        slot_in = lax.dot_general(dispatch, block_rows, (((0,), (0,)), ((), ())), preferred_element_type=jnp.float32).astype(jnp.bfloat16)
        slot_in = jnp.repeat(slot_in.reshape(EXPERTS, SLOTS, features), splits, axis=0)
        hidden = jax.nn.gelu(jnp.einsum('esd,edh->esh', slot_in.astype(jnp.float32), w_in.astype(jnp.float32))).astype(jnp.bfloat16)
        partial_out = jnp.einsum('esh,ehd->esd', hidden.astype(jnp.float32), w_out.astype(jnp.float32)).astype(jnp.bfloat16)
        outputs = lax.optimization_barrier(jnp.sum(partial_out.astype(jnp.float32).reshape(EXPERTS, splits, SLOTS, features), axis=1))
        outputs = outputs.astype(jnp.bfloat16).reshape(EXPERTS * SLOTS, features)
        combine = softmax_rows(logits, 1)
        return jnp.dot(combine, outputs, preferred_element_type=jnp.float32)
    moe_out = lax.map(per_block, blocks).reshape(frame_count * pos_count, features)
    frames_out = (residual.astype(jnp.float32) + moe_out).astype(jnp.bfloat16)
    return frames_out.reshape(frame_count, pos_count, features)
```

```python
import functools

import jax
import jax.numpy as jnp
from jax import lax
from jax.experimental import pallas as pl
from jax.experimental.pallas import tpu as pltpu
from jax.sharding import PartitionSpec as P

HEADS = 8
EXPERTS = 16
SLOTS = 64


EPS = 1e-06
LOGIT_SCALE = 3.0
MASKED = -1e30


def joined(shard, axis, combine):
    everything = jax.tree.map(lambda part: lax.all_gather(part, axis), shard)
    leading = jax.tree.map(lambda part: part[0], everything)

    def hop(k, so_far):
        return combine(so_far, jax.tree.map(lambda part: part[k], everything))

    return lax.fori_loop(1, lax.axis_size(axis), hop, leading)


def from_partner(block, axis, apart):
    count = lax.axis_size(axis)
    route = []
    for low in range(count):
        high = low | 1 << apart
        if high != low and high < count:
            route += [(low, high), (high, low)]
    return lax.ppermute(block, axis, route)


def rms_scale(values_in, gain):
    values_in = values_in.astype(jnp.float32)
    mean_sq = jnp.mean(values_in * values_in, axis=-1, keepdims=True)
    return values_in * lax.rsqrt(mean_sq + EPS) * gain


def softmax_rows(scores, axis_index):
    largest = jnp.max(scores, axis=axis_index, keepdims=True)
    weights = jnp.exp(scores - largest)
    return (weights / jnp.sum(weights, axis=axis_index, keepdims=True)).astype(jnp.bfloat16)


def merge_stats(first_pair, second_pair):
    largest = jnp.maximum(first_pair[0], second_pair[0])
    totals = first_pair[1] * jnp.exp(first_pair[0] - largest) + second_pair[1] * jnp.exp(
        second_pair[0] - largest
    )
    return (largest, totals)


def moe_plain(residual, moe_gain, dispatch_keys, w_in, w_out):
    features = residual.shape[1]
    moe_input = rms_scale(residual, moe_gain).astype(jnp.bfloat16)
    logits = LOGIT_SCALE * jnp.dot(moe_input, dispatch_keys, preferred_element_type=jnp.float32)
    local_max = jnp.max(logits, axis=0)
    local_sum = jnp.sum(jnp.exp(logits - local_max[None, :]), axis=0)
    largest, totals = joined((local_max, local_sum), "pos", merge_stats)
    dispatch = (jnp.exp(logits - largest[None, :]) / totals[None, :]).astype(jnp.bfloat16)
    count_pos = lax.axis_size("pos")
    position = lax.axis_index("pos")
    splits = max(1, count_pos // EXPERTS)
    split_bits = splits.bit_length() - 1
    pieces_dev = EXPERTS * splits // count_pos
    local_experts = max(1, pieces_dev // splits)
    slot_partial = lax.dot_general(
        dispatch, moe_input, (((0,), (0,)), ((), ())), preferred_element_type=jnp.float32
    )
    slot_totals = lax.psum(slot_partial.astype(jnp.bfloat16), "pos").astype(jnp.float32)
    first_row = position * pieces_dev // splits * SLOTS
    slot_in = lax.dynamic_slice_in_dim(slot_totals, first_row, local_experts * SLOTS, 0).astype(
        jnp.bfloat16
    )
    slot_in = slot_in.reshape(local_experts, SLOTS, features)
    hidden = jax.nn.gelu(
        jnp.einsum("esd,edh->esh", slot_in, w_in, preferred_element_type=jnp.float32)
    ).astype(jnp.bfloat16)
    partial_out = jnp.einsum(
        "esh,ehd->esd", hidden, w_out, preferred_element_type=jnp.float32
    ).astype(jnp.bfloat16)
    shares = partial_out.astype(jnp.float32).reshape(pieces_dev * SLOTS, features)
    for bit_index in reversed(range(split_bits)):
        half_rows = shares.shape[0] // 2
        lower_half = shares[:half_rows]
        upper_half = shares[half_rows:]
        upper_bit = position // 2**bit_index % 2 == 1
        kept_rows = jnp.where(upper_bit, upper_half, lower_half)
        sent_rows = jnp.where(upper_bit, lower_half, upper_half)
        shares = kept_rows + from_partner(sent_rows.astype(jnp.bfloat16), "pos", bit_index).astype(
            sent_rows.dtype
        )
    outputs = shares.astype(jnp.bfloat16)
    combine = softmax_rows(logits, 1)
    moe_out = jnp.dot(
        combine,
        lax.all_gather(outputs, "pos", axis=0, tiled=True),
        preferred_element_type=jnp.float32,
    )
    frames_out = (residual.astype(jnp.float32) + moe_out).astype(jnp.bfloat16)
    return frames_out


MESH = pl.DeviceIdType.MESH
NT = (((1,), (1,)), ((), ()))
LANES = 128


def attention_kernel(
    count, heads, x_ref, gain_ref, wq_ref, wk_ref, wv_ref, wo_ref, out_ref,
    normed, spread, mixed, home, in_send, in_recv, out_send, out_recv,
):
    me = lax.axis_index("frame")
    steps, _, frames, features = x_ref.shape
    rows = count * frames
    head_dim = features // heads
    per_group = max(1, LANES // head_dim)
    width = per_group * head_dim
    scale = head_dim ** (-0.5)

    barrier = pltpu.get_barrier_semaphore()
    for k in range(1, count):
        peer = lax.rem(me + k, count)
        pl.semaphore_signal(barrier, inc=1, device_id={"frame": peer}, device_id_type=MESH)
    pl.semaphore_wait(barrier, count - 1)

    def copy_in(i, target, source):
        return pltpu.make_async_remote_copy(
            src_ref=normed.at[i, target], dst_ref=spread.at[i, source],
            send_sem=in_send.at[i, target], recv_sem=in_recv.at[i, source],
            device_id={"frame": target}, device_id_type=MESH,
        )

    def copy_back(i, target, source):
        return pltpu.make_async_remote_copy(
            src_ref=mixed.at[i, target], dst_ref=home.at[i, source],
            send_sem=out_send.at[i, target], recv_sem=out_recv.at[i, source],
            device_id={"frame": target}, device_id_type=MESH,
        )

    def norm_step(i, carry):
        values = x_ref[i].reshape(rows, features)
        normed[i] = rms_scale(values, gain_ref[...]).astype(jnp.bfloat16).reshape(
            count, frames, features
        )
        for k in range(1, count):
            copy_in(i, lax.rem(me + k, count), me).start()
        spread[i, me] = normed[i, me]
        return carry

    lax.fori_loop(0, steps, norm_step, 0)

    def attend_step(i, carry):
        for k in range(1, count):
            peer = lax.rem(me + k, count)
            copy_in(i, peer, peer).wait_recv()
        tokens = spread[i].reshape(rows, features)
        queries = jnp.dot(tokens, wq_ref[...], preferred_element_type=jnp.float32).astype(jnp.bfloat16)
        keys = jnp.dot(tokens, wk_ref[...], preferred_element_type=jnp.float32).astype(jnp.bfloat16)
        values = jnp.dot(tokens, wv_ref[...], preferred_element_type=jnp.float32).astype(jnp.bfloat16)
        causal = lax.broadcasted_iota(jnp.int32, (rows, rows), 0) >= lax.broadcasted_iota(
            jnp.int32, (rows, rows), 1
        )
        lane_head = lax.broadcasted_iota(jnp.int32, (1, width), 1) // head_dim
        for group in range(features // width):
            lanes = slice(group * width, (group + 1) * width)
            total = jnp.zeros((rows, width), jnp.float32)
            for j in range(per_group):
                chosen = (lane_head == j).astype(jnp.float32)
                scores = lax.dot_general(
                    queries[:, lanes] * chosen.astype(jnp.bfloat16), keys[:, lanes], NT,
                    preferred_element_type=jnp.float32,
                ) * scale
                scores = jnp.where(causal, scores, MASKED)
                weights = jnp.exp(scores - jnp.max(scores, axis=1, keepdims=True))
                sums = jnp.sum(weights, axis=1, keepdims=True)
                part = jnp.dot(
                    weights.astype(jnp.bfloat16), values[:, lanes], preferred_element_type=jnp.float32
                )
                total = total + part * (chosen / sums)
            mixed[i, :, :, lanes] = total.astype(jnp.bfloat16).reshape(count, frames, width)
        for k in range(1, count):
            copy_back(i, lax.rem(me + k, count), me).start()
        home[i, me] = mixed[i, me]
        return carry

    lax.fori_loop(0, steps, attend_step, 0)

    def output_step(i, carry):
        for k in range(1, count):
            peer = lax.rem(me + k, count)
            copy_back(i, peer, peer).wait_recv()
        result = x_ref[i].reshape(rows, features).astype(jnp.float32) + jnp.dot(
            home[i].reshape(rows, features), wo_ref[...], preferred_element_type=jnp.float32
        )
        out_ref[i] = result.astype(jnp.bfloat16).reshape(count, frames, features)
        return carry

    lax.fori_loop(0, steps, output_step, 0)

    def drain_step(i, carry):
        for k in range(1, count):
            peer = lax.rem(me + k, count)
            copy_in(i, peer, me).wait_send()
            copy_back(i, peer, me).wait_send()
        return carry

    lax.fori_loop(0, steps, drain_step, 0)


def attention_block(x, gain, w_query, w_key, w_value, w_output):
    count = lax.axis_size("frame")
    steps = x.shape[0]
    vmem = pl.BlockSpec(memory_space=pltpu.VMEM)
    buffer = pltpu.VMEM(x.shape, jnp.bfloat16)
    sems = pltpu.SemaphoreType.DMA((steps, count))
    return pl.pallas_call(
        functools.partial(attention_kernel, count, HEADS),
        out_shape=jax.ShapeDtypeStruct(x.shape, jnp.bfloat16),
        in_specs=[vmem] * 6,
        out_specs=vmem,
        scratch_shapes=[buffer] * 4 + [sems] * 4,
        compiler_params=pltpu.CompilerParams(
            collective_id=0, has_side_effects=True, vmem_limit_bytes=48 * 2**20
        ),
    )(x, gain.reshape(1, -1), w_query, w_key, w_value, w_output)


def moe_kernel(
    count, res_ref, gain_ref, keys_ref, keys_t_ref, w_in_hbm, w_out_hbm, out_ref,
    tokens, comb, part, part_stat, exch, exch_stat, merged, merged_stat, recv, recv_stat,
    w_in, w_out, outs, total,
    w_sem, x_send, x_recv, xs_send, xs_recv, m_send, m_recv, ms_send, ms_recv,
    g_send, g_recv, f_send, f_recv,
):
    pos = lax.axis_index("pos")
    chips = count // 2
    chip, core = pos // 2, lax.rem(pos, 2)
    partner = chip * 2 + 1 - core
    rows_dev = outs.shape[1]
    rows_chip = 2 * rows_dev
    token_count, features = res_ref.shape
    last = chips - 1

    load_in = pltpu.make_async_copy(w_in_hbm, w_in, w_sem.at[0])
    load_out = pltpu.make_async_copy(w_out_hbm, w_out, w_sem.at[1])
    load_in.start()
    load_out.start()

    barrier = pltpu.get_barrier_semaphore()
    for k in range(1, chips):
        peer = lax.rem(chip + k, chips) * 2 + core
        pl.semaphore_signal(barrier, inc=1, device_id={"pos": peer}, device_id_type=MESH)
    pl.semaphore_signal(barrier, inc=1, device_id={"pos": partner}, device_id_type=MESH)
    pl.semaphore_wait(barrier, chips)

    tile = min(256, token_count)
    tiles = token_count // tile

    def tile_rows(t):
        return pl.ds(pl.multiple_of(t * tile, tile), tile)

    def norm_step(t, carry):
        block = tile_rows(t)
        tokens[block] = rms_scale(res_ref[block], gain_ref[...]).astype(jnp.bfloat16)
        return carry

    lax.fori_loop(0, tiles, norm_step, 0)

    eye = lax.broadcasted_iota(jnp.int32, (rows_dev, rows_dev), 0) == lax.broadcasted_iota(
        jnp.int32, (rows_dev, rows_dev), 1
    )

    def as_row(column):
        return jnp.sum(jnp.where(eye, column, 0.0), axis=0, keepdims=True)

    def as_column(row):
        return jnp.sum(jnp.where(eye, row, 0.0), axis=1, keepdims=True)

    def pair(src, dst, sends, recvs, k, target):
        return pltpu.make_async_remote_copy(
            src_ref=src, dst_ref=dst, send_sem=sends.at[k], recv_sem=recvs.at[k],
            device_id={"pos": target}, device_id_type=MESH,
        )

    def exchange(k):
        return (
            pair(part.at[k, 1 - core], exch.at[k], x_send, x_recv, k, partner),
            pair(part_stat.at[k, 1 - core], exch_stat.at[k], xs_send, xs_recv, k, partner),
        )

    def scatter(k):
        target = lax.rem(chip + last - k, chips) * 2 + core
        return (
            pair(merged.at[k], recv.at[k], m_send, m_recv, k, target),
            pair(merged_stat.at[k], recv_stat.at[k], ms_send, ms_recv, k, target),
        )

    def dispatch(k):
        target = lax.rem(chip + last - k, chips)
        chunk = keys_t_ref[pl.ds(pl.multiple_of(target * rows_chip, rows_chip), rows_chip)]
        logits = LOGIT_SCALE * lax.dot_general(
            chunk, tokens[...], NT, preferred_element_type=jnp.float32
        )
        largest = jnp.max(logits, axis=1, keepdims=True)
        weights = jnp.exp(logits - largest)
        sums = jnp.sum(weights, axis=1, keepdims=True)
        sent = jnp.dot(
            weights.astype(jnp.bfloat16), tokens[...], preferred_element_type=jnp.float32
        ).astype(jnp.bfloat16)
        for c in range(2):
            own = slice(c * rows_dev, (c + 1) * rows_dev)
            part[k, c] = sent[own]
            part_stat[k, c, 0:1, :] = as_row(largest[own])
            part_stat[k, c, 1:2, :] = as_row(sums[own])
        for copy in exchange(k):
            copy.start()

    def merge_pair(k):
        for copy in exchange(k):
            copy.wait_recv()
        mine, other = part_stat[k, core], exch_stat[k]
        largest = jnp.maximum(mine[0:1], other[0:1])
        scale_mine = jnp.exp(mine[0:1] - largest)
        scale_other = jnp.exp(other[0:1] - largest)
        merged_stat[k, 0:1, :] = largest
        merged_stat[k, 1:2, :] = mine[1:2] * scale_mine + other[1:2] * scale_other
        merged[k] = (
            part[k, core].astype(jnp.float32) * as_column(scale_mine)
            + exch[k].astype(jnp.float32) * as_column(scale_other)
        ).astype(jnp.bfloat16)

    part_stat[...] = jnp.zeros_like(part_stat)
    merged_stat[...] = jnp.zeros_like(merged_stat)

    def dispatch_step(k, carry):
        dispatch(k)

        @pl.when(k >= 1)
        def _():
            merge_pair(k - 1)
            for copy in scatter(k - 1):
                copy.start()

        return carry

    lax.fori_loop(0, chips, dispatch_step, 0)

    def combine_step(t, carry):
        block = tile_rows(t)
        logits = LOGIT_SCALE * jnp.dot(
            tokens[block], keys_ref[...], preferred_element_type=jnp.float32
        )
        weights = jnp.exp(logits - jnp.max(logits, axis=1, keepdims=True))
        weights = (weights / jnp.sum(weights, axis=1, keepdims=True)).astype(jnp.bfloat16)
        for c in range(chips):
            comb[c, block] = weights[:, c * rows_chip : (c + 1) * rows_chip]
        return carry

    lax.fori_loop(0, tiles, combine_step, 0)

    merge_pair(last)
    for k in range(last):
        for copy in scatter(k):
            copy.wait_recv()
    stats = [recv_stat[k] for k in range(last)] + [merged_stat[last]]
    blocks = [recv[k] for k in range(last)] + [merged[last]]
    largest = functools.reduce(jnp.maximum, [stat[0:1] for stat in stats])
    scales = [jnp.exp(stat[0:1] - largest) for stat in stats]
    sums = sum(stat[1:2] * scale for stat, scale in zip(stats, scales))
    slot_in = sum(
        block.astype(jnp.float32) * as_column(scale / sums) for block, scale in zip(blocks, scales)
    ).astype(jnp.bfloat16)

    load_in.wait()
    load_out.wait()
    for e in range(w_in.shape[0]):
        own = slice(e * SLOTS, (e + 1) * SLOTS)
        hidden = jax.nn.gelu(
            jnp.dot(slot_in[own], w_in[e], preferred_element_type=jnp.float32)
        ).astype(jnp.bfloat16)
        outs[pos, own] = jnp.dot(hidden, w_out[e], preferred_element_type=jnp.float32).astype(
            jnp.bfloat16
        )

    def gather(k, target, source):
        return pair(outs.at[source], outs.at[source], g_send, g_recv, k, target)

    def forward(k, source):
        return pair(outs.at[source], outs.at[source], f_send, f_recv, k, partner)

    def chip_at(k):
        return lax.rem(chip + chips - k, chips)

    for k in range(1, chips):
        gather(k, lax.rem(chip + k, chips) * 2 + core, pos).start()
    forward(0, pos).start()

    def add_chip(k, source, first, final):
        pair_rows = outs[pl.ds(source * 2, 2)].reshape(rows_chip, features)

        def add_step(t, carry):
            block = tile_rows(t)
            before = res_ref[block].astype(jnp.float32) if first else total[block]
            result = before + jnp.dot(
                comb[source, block], pair_rows, preferred_element_type=jnp.float32
            )
            if final:
                out_ref[block] = result.astype(jnp.bfloat16)
            else:
                total[block] = result
            return carry

        lax.fori_loop(0, tiles, add_step, 0)

    order = sorted(range(1, chips), key=lambda k: min(k, chips - k))
    forward(0, partner).wait_recv()
    waiting = 0
    for step, k in enumerate(order + [None]):
        if k is not None:
            source = chip_at(k) * 2 + core
            gather(k, pos, source).wait_recv()
            forward(k, source).start()
        add_chip(waiting, chip_at(waiting), step == 0, k is None)
        if k is not None:
            forward(k, chip_at(k) * 2 + 1 - core).wait_recv()
            waiting = k

    for k in range(chips):
        for copy in exchange(k):
            copy.wait_send()
        forward(k, pos).wait_send()
    for k in range(last):
        for copy in scatter(k):
            copy.wait_send()
        gather(k + 1, pos, pos).wait_send()


def moe_block(residual, gain, dispatch_keys, w_in, w_out):
    count = lax.axis_size("pos")
    chips = count // 2
    token_count, features = residual.shape
    slots = dispatch_keys.shape[1]
    rows_dev = slots // count
    vmem = pl.BlockSpec(memory_space=pltpu.VMEM)
    anywhere = pl.BlockSpec(memory_space=pl.ANY)
    half = jnp.bfloat16

    def rows(*lead):
        return pltpu.VMEM(lead + (rows_dev, features), half)

    def stat(*lead):
        return pltpu.VMEM(lead + (8, rows_dev), jnp.float32)

    sems = pltpu.SemaphoreType.DMA((chips,))
    return pl.pallas_call(
        functools.partial(moe_kernel, count),
        out_shape=jax.ShapeDtypeStruct(residual.shape, half),
        in_specs=[vmem] * 4 + [anywhere] * 2,
        out_specs=vmem,
        scratch_shapes=[
            pltpu.VMEM((token_count, features), half),
            pltpu.VMEM((chips, token_count, 2 * rows_dev), half),
            rows(chips, 2), stat(chips, 2), rows(chips), stat(chips),
            rows(chips), stat(chips), rows(chips), stat(chips),
            pltpu.VMEM(w_in.shape, half), pltpu.VMEM(w_out.shape, half),
            rows(count), pltpu.VMEM((token_count, features), jnp.float32),
            pltpu.SemaphoreType.DMA((2,)),
        ] + [sems] * 12,
        compiler_params=pltpu.CompilerParams(
            collective_id=1, has_side_effects=True, vmem_limit_bytes=56 * 2**20
        ),
    )(residual, gain.reshape(1, -1), dispatch_keys, dispatch_keys.T, w_in, w_out)


def local(
    frames_in, attn_gain, w_query, w_key, w_value, w_output, moe_gain, dispatch_keys, w_in, w_out
):
    frame_count, pos_count, features = frames_in.shape
    blocks = lax.axis_size("frame")
    steps = pos_count // blocks
    x = frames_in.reshape(frame_count, blocks, steps, features).transpose(2, 1, 0, 3)
    residual = attention_block(x, attn_gain, w_query, w_key, w_value, w_output)
    residual = residual.reshape(frame_count * pos_count, features)
    count_pos = lax.axis_size("pos")
    whole_experts = w_in.shape[0] * count_pos == EXPERTS and count_pos % 2 == 0
    if whole_experts and dispatch_keys.shape[1] // count_pos % LANES == 0:
        frames_out = moe_block(residual, moe_gain, dispatch_keys, w_in, w_out)
    else:
        frames_out = moe_plain(residual, moe_gain, dispatch_keys, w_in, w_out)
    frames_out = frames_out.reshape(steps, blocks, frame_count, features)
    return frames_out.transpose(2, 1, 0, 3).reshape(frame_count, pos_count, features)


def solution(mesh):
    in_specs = (
        P("frame", "pos", None),
        P(),
        P(),
        P(),
        P(),
        P(),
        P(),
        P(),
        P("pos", None, None),
        P("pos", None, None),
    )
    out_specs = P("frame", "pos", None)
    return jax.shard_map(local, mesh=mesh, in_specs=in_specs, out_specs=out_specs, check_vma=False)
```

```python
import functools

import jax
import jax.numpy as jnp
from jax import lax
from jax.experimental import pallas as pl
from jax.experimental.pallas import tpu as pltpu
from jax.sharding import PartitionSpec as P

HEADS = 8
EXPERTS = 16
SLOTS = 64


EPS = 1e-06
LOGIT_SCALE = 3.0
MASKED = -1e30


def joined(shard, axis, combine):
    everything = jax.tree.map(lambda part: lax.all_gather(part, axis), shard)
    leading = jax.tree.map(lambda part: part[0], everything)

    def hop(k, so_far):
        return combine(so_far, jax.tree.map(lambda part: part[k], everything))

    return lax.fori_loop(1, lax.axis_size(axis), hop, leading)


def from_partner(block, axis, apart):
    count = lax.axis_size(axis)
    route = []
    for low in range(count):
        high = low | 1 << apart
        if high != low and high < count:
            route += [(low, high), (high, low)]
    return lax.ppermute(block, axis, route)


def rms_scale(values_in, gain):
    values_in = values_in.astype(jnp.float32)
    mean_sq = jnp.mean(values_in * values_in, axis=-1, keepdims=True)
    return values_in * lax.rsqrt(mean_sq + EPS) * gain


def softmax_rows(scores, axis_index):
    largest = jnp.max(scores, axis=axis_index, keepdims=True)
    weights = jnp.exp(scores - largest)
    return (weights / jnp.sum(weights, axis=axis_index, keepdims=True)).astype(jnp.bfloat16)


def merge_stats(first_pair, second_pair):
    largest = jnp.maximum(first_pair[0], second_pair[0])
    totals = first_pair[1] * jnp.exp(first_pair[0] - largest) + second_pair[1] * jnp.exp(
        second_pair[0] - largest
    )
    return (largest, totals)


def moe_plain(residual, moe_gain, dispatch_keys, w_in, w_out):
    features = residual.shape[1]
    moe_input = rms_scale(residual, moe_gain).astype(jnp.bfloat16)
    logits = LOGIT_SCALE * jnp.dot(moe_input, dispatch_keys, preferred_element_type=jnp.float32)
    local_max = jnp.max(logits, axis=0)
    local_sum = jnp.sum(jnp.exp(logits - local_max[None, :]), axis=0)
    largest, totals = joined((local_max, local_sum), "pos", merge_stats)
    dispatch = (jnp.exp(logits - largest[None, :]) / totals[None, :]).astype(jnp.bfloat16)
    count_pos = lax.axis_size("pos")
    position = lax.axis_index("pos")
    splits = max(1, count_pos // EXPERTS)
    split_bits = splits.bit_length() - 1
    pieces_dev = EXPERTS * splits // count_pos
    local_experts = max(1, pieces_dev // splits)
    slot_partial = lax.dot_general(
        dispatch, moe_input, (((0,), (0,)), ((), ())), preferred_element_type=jnp.float32
    )
    slot_totals = lax.psum(slot_partial.astype(jnp.bfloat16), "pos").astype(jnp.float32)
    first_row = position * pieces_dev // splits * SLOTS
    slot_in = lax.dynamic_slice_in_dim(slot_totals, first_row, local_experts * SLOTS, 0).astype(
        jnp.bfloat16
    )
    slot_in = slot_in.reshape(local_experts, SLOTS, features)
    hidden = jax.nn.gelu(
        jnp.einsum("esd,edh->esh", slot_in, w_in, preferred_element_type=jnp.float32)
    ).astype(jnp.bfloat16)
    partial_out = jnp.einsum(
        "esh,ehd->esd", hidden, w_out, preferred_element_type=jnp.float32
    ).astype(jnp.bfloat16)
    shares = partial_out.astype(jnp.float32).reshape(pieces_dev * SLOTS, features)
    for bit_index in reversed(range(split_bits)):
        half_rows = shares.shape[0] // 2
        lower_half = shares[:half_rows]
        upper_half = shares[half_rows:]
        upper_bit = position // 2**bit_index % 2 == 1
        kept_rows = jnp.where(upper_bit, upper_half, lower_half)
        sent_rows = jnp.where(upper_bit, lower_half, upper_half)
        shares = kept_rows + from_partner(sent_rows.astype(jnp.bfloat16), "pos", bit_index).astype(
            sent_rows.dtype
        )
    outputs = shares.astype(jnp.bfloat16)
    combine = softmax_rows(logits, 1)
    moe_out = jnp.dot(
        combine,
        lax.all_gather(outputs, "pos", axis=0, tiled=True),
        preferred_element_type=jnp.float32,
    )
    frames_out = (residual.astype(jnp.float32) + moe_out).astype(jnp.bfloat16)
    return frames_out


MESH = pl.DeviceIdType.MESH
NT = (((1,), (1,)), ((), ()))
LANES = 128


def greet(peers):
    barrier = pltpu.get_barrier_semaphore()
    for peer in peers:
        pl.semaphore_signal(barrier, inc=1, device_id=peer, device_id_type=MESH)
    pl.semaphore_wait(barrier, len(peers))


def frame_peers(count):
    me = lax.axis_index("frame")
    return [{"frame": lax.rem(me + k, count)} for k in range(1, count)]


def attention_phases(
    count, heads, load_x, load_weights, emit_tile,
    x_ref, gain_ref, wq_ref, wk_ref, wv_ref, wo_ref,
    normed, spread, mixed, home, in_send, in_recv, out_send, out_recv,
):
    me = lax.axis_index("frame")
    steps, _, frames, features = x_ref.shape
    rows = count * frames
    head_dim = features // heads
    per_group = max(1, LANES // head_dim)
    width = per_group * head_dim
    scale = head_dim ** (-0.5)

    def copy_in(i, target, source):
        return pltpu.make_async_remote_copy(
            src_ref=normed.at[i, target], dst_ref=spread.at[i, source],
            send_sem=in_send.at[i, target], recv_sem=in_recv.at[i, source],
            device_id={"frame": target}, device_id_type=MESH,
        )

    def copy_back(i, target, source):
        return pltpu.make_async_remote_copy(
            src_ref=mixed.at[i, target], dst_ref=home.at[i, source],
            send_sem=out_send.at[i, target], recv_sem=out_recv.at[i, source],
            device_id={"frame": target}, device_id_type=MESH,
        )

    def norm_step(i, carry):
        load_x(i)
        values = x_ref[i].reshape(rows, features)
        normed[i] = rms_scale(values, gain_ref[...]).astype(jnp.bfloat16).reshape(
            count, frames, features
        )
        for k in range(1, count):
            copy_in(i, lax.rem(me + k, count), me).start()
        spread[i, me] = normed[i, me]
        return carry

    lax.fori_loop(0, steps, norm_step, 0)
    load_weights()

    def attend_step(i, carry):
        for k in range(1, count):
            peer = lax.rem(me + k, count)
            copy_in(i, peer, peer).wait_recv()
        tokens = spread[i].reshape(rows, features)
        queries = jnp.dot(tokens, wq_ref[...], preferred_element_type=jnp.float32).astype(jnp.bfloat16)
        keys = jnp.dot(tokens, wk_ref[...], preferred_element_type=jnp.float32).astype(jnp.bfloat16)
        values = jnp.dot(tokens, wv_ref[...], preferred_element_type=jnp.float32).astype(jnp.bfloat16)
        causal = lax.broadcasted_iota(jnp.int32, (rows, rows), 0) >= lax.broadcasted_iota(
            jnp.int32, (rows, rows), 1
        )
        lane_head = lax.broadcasted_iota(jnp.int32, (1, width), 1) // head_dim
        for group in range(features // width):
            lanes = slice(group * width, (group + 1) * width)
            total = jnp.zeros((rows, width), jnp.float32)
            for j in range(per_group):
                chosen = (lane_head == j).astype(jnp.float32)
                scores = lax.dot_general(
                    queries[:, lanes] * chosen.astype(jnp.bfloat16), keys[:, lanes], NT,
                    preferred_element_type=jnp.float32,
                ) * scale
                scores = jnp.where(causal, scores, MASKED)
                weights = jnp.exp(scores - jnp.max(scores, axis=1, keepdims=True))
                sums = jnp.sum(weights, axis=1, keepdims=True)
                part = jnp.dot(
                    weights.astype(jnp.bfloat16), values[:, lanes], preferred_element_type=jnp.float32
                )
                total = total + part * (chosen / sums)
            mixed[i, :, :, lanes] = total.astype(jnp.bfloat16).reshape(count, frames, width)
        for k in range(1, count):
            copy_back(i, lax.rem(me + k, count), me).start()
        home[i, me] = mixed[i, me]
        return carry

    lax.fori_loop(0, steps, attend_step, 0)

    def output_step(i, carry):
        for k in range(1, count):
            peer = lax.rem(me + k, count)
            copy_back(i, peer, peer).wait_recv()
        result = x_ref[i].reshape(rows, features).astype(jnp.float32) + jnp.dot(
            home[i].reshape(rows, features), wo_ref[...], preferred_element_type=jnp.float32
        )
        emit_tile(i, result.astype(jnp.bfloat16))
        return carry

    lax.fori_loop(0, steps, output_step, 0)

    def drain_step(i, carry):
        for k in range(1, count):
            peer = lax.rem(me + k, count)
            copy_in(i, peer, me).wait_send()
            copy_back(i, peer, me).wait_send()
        return carry

    return lambda: lax.fori_loop(0, steps, drain_step, 0)


def attention_kernel(
    count, heads, x_ref, gain_ref, wq_ref, wk_ref, wv_ref, wo_ref, out_ref, *scratch
):
    greet(frame_peers(count))

    def emit_tile(i, result):
        out_ref[i] = result.reshape(out_ref.shape[1:])

    attention_phases(
        count, heads, lambda i: None, lambda: None, emit_tile,
        x_ref, gain_ref, wq_ref, wk_ref, wv_ref, wo_ref, *scratch,
    )()


def attention_block(x, gain, w_query, w_key, w_value, w_output):
    count = lax.axis_size("frame")
    steps = x.shape[0]
    vmem = pl.BlockSpec(memory_space=pltpu.VMEM)
    buffer = pltpu.VMEM(x.shape, jnp.bfloat16)
    sems = pltpu.SemaphoreType.DMA((steps, count))
    return pl.pallas_call(
        functools.partial(attention_kernel, count, HEADS),
        out_shape=jax.ShapeDtypeStruct(x.shape, jnp.bfloat16),
        in_specs=[vmem] * 6,
        out_specs=vmem,
        scratch_shapes=[buffer] * 4 + [sems] * 4,
        compiler_params=pltpu.CompilerParams(
            collective_id=1, has_side_effects=True, vmem_limit_bytes=48 * 2**20
        ),
    )(x, gain.reshape(1, -1), w_query, w_key, w_value, w_output)


def layer_kernel(
    frames, count, heads,
    x_hbm, gain_ref, moe_gain_ref, wq_hbm, wk_hbm, wv_hbm, wo_hbm, keys_hbm, w_in_hbm, w_out_hbm,
    out_ref,
    x_ref, wq, wk, wv, wo, keys_ref, w_in, w_out, x_sem, w_sem,
    normed, spread, mixed, home, in_send, in_recv, out_send, out_recv,
    keys_t, res_ref, tokens, comb, slot_sum, slot_max, slot_total,
    part, part_stat, exch, exch_stat, merged, merged_stat, recv, recv_stat,
    outs, total,
    x_send, x_recv, xs_send, xs_recv, m_send, m_recv, ms_send, ms_recv,
    g_send, g_recv, f_send, f_recv,
):
    steps = x_ref.shape[0]
    pos = lax.axis_index("pos")
    chips = count // 2
    chip, core = pos // 2, lax.rem(pos, 2)
    partner = chip * 2 + 1 - core
    rows_dev = outs.shape[1]
    rows_chip = 2 * rows_dev
    token_count, features = res_ref.shape
    last = chips - 1
    tiles = steps
    tile = token_count // tiles

    def load_step(i, carry):
        pltpu.make_async_copy(x_hbm.at[i], x_ref.at[i], x_sem.at[i]).start()
        return carry

    lax.fori_loop(0, steps, load_step, 0)
    early = [
        pltpu.make_async_copy(src, dst, w_sem.at[n])
        for n, (src, dst) in enumerate(
            ((wq_hbm, wq), (wk_hbm, wk), (wv_hbm, wv), (wo_hbm, wo), (keys_hbm, keys_ref))
        )
    ]
    late = [
        pltpu.make_async_copy(src, dst, w_sem.at[len(early) + n])
        for n, (src, dst) in enumerate(((w_in_hbm, w_in), (w_out_hbm, w_out)))
    ]
    for copy in early:
        copy.start()

    greet(
        frame_peers(frames)
        + [{"pos": lax.rem(chip + k, chips) * 2 + core} for k in range(1, chips)]
        + [{"pos": partner}]
    )

    def load_x(i):
        pltpu.make_async_copy(x_hbm.at[i], x_ref.at[i], x_sem.at[i]).wait()

    def load_weights():
        for copy in late:
            copy.start()
        for copy in early:
            copy.wait()
        for c in range(keys_t.shape[0] // LANES):
            own = slice(c * LANES, (c + 1) * LANES)
            keys_t[own] = keys_ref[:, own].T

    def tile_rows(t):
        return pl.ds(pl.multiple_of(t * tile, tile), tile)

    eye = lax.broadcasted_iota(jnp.int32, (rows_dev, rows_dev), 0) == lax.broadcasted_iota(
        jnp.int32, (rows_dev, rows_dev), 1
    )

    def as_row(column):
        return jnp.sum(jnp.where(eye, column, 0.0), axis=0, keepdims=True)

    def as_column(row):
        return jnp.sum(jnp.where(eye, row, 0.0), axis=1, keepdims=True)

    def pair(src, dst, sends, recvs, k, target):
        return pltpu.make_async_remote_copy(
            src_ref=src, dst_ref=dst, send_sem=sends.at[k], recv_sem=recvs.at[k],
            device_id={"pos": target}, device_id_type=MESH,
        )

    def exchange(k):
        return (
            pair(part.at[k, 1 - core], exch.at[k], x_send, x_recv, k, partner),
            pair(part_stat.at[k, 1 - core], exch_stat.at[k], xs_send, xs_recv, k, partner),
        )

    def scatter(k):
        target = lax.rem(chip + last - k, chips) * 2 + core
        return (
            pair(merged.at[k], recv.at[k], m_send, m_recv, k, target),
            pair(merged_stat.at[k], recv_stat.at[k], ms_send, ms_recv, k, target),
        )

    part_stat[...] = jnp.zeros_like(part_stat)
    merged_stat[...] = jnp.zeros_like(merged_stat)
    slot_sum[...] = jnp.zeros_like(slot_sum)
    slot_total[...] = jnp.zeros_like(slot_total)
    slot_max[...] = jnp.full_like(slot_max, MASKED)

    def add_tile(t, c):
        block = tokens[tile_rows(t)]
        logits = LOGIT_SCALE * lax.dot_general(
            keys_t[pl.ds(pl.multiple_of(c * rows_chip, rows_chip), rows_chip)], block, NT,
            preferred_element_type=jnp.float32,
        )
        before = slot_max[c]
        largest = jnp.maximum(before, jnp.max(logits, axis=1, keepdims=True))
        weights = jnp.exp(logits - largest)
        fade = jnp.exp(before - largest)
        sums = slot_total[c] * fade + jnp.sum(weights, axis=1, keepdims=True)
        summed = slot_sum[c] * fade + jnp.dot(
            weights.astype(jnp.bfloat16), block, preferred_element_type=jnp.float32
        )
        return largest, sums, summed

    def combine_tile(t):
        block = tile_rows(t)
        logits = LOGIT_SCALE * jnp.dot(
            tokens[block], keys_ref[...], preferred_element_type=jnp.float32
        )
        weights = jnp.exp(logits - jnp.max(logits, axis=1, keepdims=True))
        weights = (weights / jnp.sum(weights, axis=1, keepdims=True)).astype(jnp.bfloat16)
        for c in range(chips):
            comb[c, block] = weights[:, c * rows_chip : (c + 1) * rows_chip]

    def emit_tile(t, result):
        block = tile_rows(t)
        res_ref[block] = result
        tokens[block] = rms_scale(result, moe_gain_ref[...]).astype(jnp.bfloat16)

        @pl.when(t < tiles - 1)
        def _():
            def chunk_step(c, carry):
                slot_max[c], slot_total[c], slot_sum[c] = add_tile(t, c)
                return carry

            lax.fori_loop(0, chips, chunk_step, 0)
            combine_tile(t)

    drain = attention_phases(
        frames, heads, load_x, load_weights, emit_tile,
        x_ref, gain_ref, wq, wk, wv, wo,
        normed, spread, mixed, home, in_send, in_recv, out_send, out_recv,
    )

    def dispatch(k):
        largest, sums, summed = add_tile(tiles - 1, lax.rem(chip + last - k, chips))
        sent = summed.astype(jnp.bfloat16)
        for c in range(2):
            own = slice(c * rows_dev, (c + 1) * rows_dev)
            part[k, c] = sent[own]
            part_stat[k, c, 0:1, :] = as_row(largest[own])
            part_stat[k, c, 1:2, :] = as_row(sums[own])
        for copy in exchange(k):
            copy.start()

    def merge_pair(k):
        for copy in exchange(k):
            copy.wait_recv()
        mine, other = part_stat[k, core], exch_stat[k]
        largest = jnp.maximum(mine[0:1], other[0:1])
        scale_mine = jnp.exp(mine[0:1] - largest)
        scale_other = jnp.exp(other[0:1] - largest)
        merged_stat[k, 0:1, :] = largest
        merged_stat[k, 1:2, :] = mine[1:2] * scale_mine + other[1:2] * scale_other
        merged[k] = (
            part[k, core].astype(jnp.float32) * as_column(scale_mine)
            + exch[k].astype(jnp.float32) * as_column(scale_other)
        ).astype(jnp.bfloat16)

    def dispatch_step(k, carry):
        dispatch(k)

        @pl.when(k >= 1)
        def _():
            merge_pair(k - 1)
            for copy in scatter(k - 1):
                copy.start()

        return carry

    lax.fori_loop(0, chips, dispatch_step, 0)

    merge_pair(last)
    combine_tile(tiles - 1)
    for k in range(last):
        for copy in scatter(k):
            copy.wait_recv()
    stats = [recv_stat[k] for k in range(last)] + [merged_stat[last]]
    blocks = [recv[k] for k in range(last)] + [merged[last]]
    largest = functools.reduce(jnp.maximum, [stat[0:1] for stat in stats])
    scales = [jnp.exp(stat[0:1] - largest) for stat in stats]
    sums = sum(stat[1:2] * scale for stat, scale in zip(stats, scales))
    slot_in = sum(
        block.astype(jnp.float32) * as_column(scale / sums) for block, scale in zip(blocks, scales)
    ).astype(jnp.bfloat16)

    for copy in late:
        copy.wait()
    for e in range(w_in.shape[0]):
        own = slice(e * SLOTS, (e + 1) * SLOTS)
        hidden = jax.nn.gelu(
            jnp.dot(slot_in[own], w_in[e], preferred_element_type=jnp.float32)
        ).astype(jnp.bfloat16)
        outs[pos, own] = jnp.dot(hidden, w_out[e], preferred_element_type=jnp.float32).astype(
            jnp.bfloat16
        )

    def gather(k, target, source):
        return pair(outs.at[source], outs.at[source], g_send, g_recv, k, target)

    def forward(k, source):
        return pair(outs.at[source], outs.at[source], f_send, f_recv, k, partner)

    def chip_at(k):
        return lax.rem(chip + chips - k, chips)

    for k in range(1, chips):
        gather(k, lax.rem(chip + k, chips) * 2 + core, pos).start()
    forward(0, pos).start()

    def add_chip(k, source, first, final):
        pair_rows = outs[pl.ds(source * 2, 2)].reshape(rows_chip, features)

        def add_step(t, carry):
            block = tile_rows(t)
            before = res_ref[block].astype(jnp.float32) if first else total[block]
            result = before + jnp.dot(
                comb[source, block], pair_rows, preferred_element_type=jnp.float32
            )
            if final:
                out_ref[block] = result.astype(jnp.bfloat16)
            else:
                total[block] = result
            return carry

        lax.fori_loop(0, tiles, add_step, 0)

    order = sorted(range(1, chips), key=lambda k: min(k, chips - k))
    forward(0, partner).wait_recv()
    waiting = 0
    for step, k in enumerate(order + [None]):
        if k is not None:
            source = chip_at(k) * 2 + core
            gather(k, pos, source).wait_recv()
            forward(k, source).start()
        add_chip(waiting, chip_at(waiting), step == 0, k is None)
        if k is not None:
            forward(k, chip_at(k) * 2 + 1 - core).wait_recv()
            waiting = k

    drain()
    for k in range(chips):
        for copy in exchange(k):
            copy.wait_send()
        forward(k, pos).wait_send()
    for k in range(last):
        for copy in scatter(k):
            copy.wait_send()
        gather(k + 1, pos, pos).wait_send()


def layer_block(
    x, attn_gain, moe_gain, w_query, w_key, w_value, w_output, dispatch_keys, w_in, w_out
):
    frames, count = lax.axis_size("frame"), lax.axis_size("pos")
    chips = count // 2
    steps, features = x.shape[0], x.shape[-1]
    token_count = x.size // features
    slots = dispatch_keys.shape[1]
    rows_dev = slots // count
    vmem = pl.BlockSpec(memory_space=pltpu.VMEM)
    anywhere = pl.BlockSpec(memory_space=pl.ANY)
    half = jnp.bfloat16

    def rows(*lead):
        return pltpu.VMEM(lead + (rows_dev, features), half)

    def stat(*lead):
        return pltpu.VMEM(lead + (8, rows_dev), jnp.float32)

    def like(array):
        return pltpu.VMEM(array.shape, half)

    sems = pltpu.SemaphoreType.DMA((chips,))
    step_sems = pltpu.SemaphoreType.DMA((steps, frames))
    column = pltpu.VMEM((chips, 2 * rows_dev, 1), jnp.float32)
    weights = (w_query, w_key, w_value, w_output, dispatch_keys, w_in, w_out)
    return pl.pallas_call(
        functools.partial(layer_kernel, frames, count, HEADS),
        out_shape=jax.ShapeDtypeStruct((token_count, features), half),
        in_specs=[anywhere] + [vmem] * 2 + [anywhere] * len(weights),
        out_specs=vmem,
        scratch_shapes=[like(x)] + [like(weight) for weight in weights]
        + [pltpu.SemaphoreType.DMA((steps,)), pltpu.SemaphoreType.DMA((len(weights),))]
        + [like(x)] * 4 + [step_sems] * 4
        + [
            pltpu.VMEM((slots, features), half),
            pltpu.VMEM((token_count, features), half),
            pltpu.VMEM((token_count, features), half),
            pltpu.VMEM((chips, token_count, 2 * rows_dev), half),
            pltpu.VMEM((chips, 2 * rows_dev, features), jnp.float32), column, column,
            rows(chips, 2), stat(chips, 2), rows(chips), stat(chips),
            rows(chips), stat(chips), rows(chips), stat(chips),
            rows(count), pltpu.VMEM((token_count, features), jnp.float32),
        ] + [sems] * 12,
        compiler_params=pltpu.CompilerParams(
            collective_id=0, has_side_effects=True, vmem_limit_bytes=60 * 2**20
        ),
    )(x, attn_gain.reshape(1, -1), moe_gain.reshape(1, -1), *weights)


def local(
    frames_in, attn_gain, w_query, w_key, w_value, w_output, moe_gain, dispatch_keys, w_in, w_out
):
    frame_count, pos_count, features = frames_in.shape
    blocks = lax.axis_size("frame")
    steps = pos_count // blocks
    x = frames_in.reshape(frame_count, blocks, steps, features).transpose(2, 1, 0, 3)
    count_pos = lax.axis_size("pos")
    whole_experts = w_in.shape[0] * count_pos == EXPERTS and count_pos % 2 == 0
    if whole_experts and dispatch_keys.shape[1] // count_pos % LANES == 0:
        frames_out = layer_block(
            x, attn_gain, moe_gain, w_query, w_key, w_value, w_output, dispatch_keys, w_in, w_out
        )
    else:
        residual = attention_block(x, attn_gain, w_query, w_key, w_value, w_output)
        residual = residual.reshape(frame_count * pos_count, features)
        frames_out = moe_plain(residual, moe_gain, dispatch_keys, w_in, w_out)
    frames_out = frames_out.reshape(steps, blocks, frame_count, features)
    return frames_out.transpose(2, 1, 0, 3).reshape(frame_count, pos_count, features)


def solution(mesh):
    in_specs = (
        P("frame", "pos", None),
        P(),
        P(),
        P(),
        P(),
        P(),
        P(),
        P(),
        P("pos", None, None),
        P("pos", None, None),
    )
    out_specs = P("frame", "pos", None)
    return jax.shard_map(local, mesh=mesh, in_specs=in_specs, out_specs=out_specs, check_vma=False)
```
